32 devices in a mesh: req: 4 (over x, core), tp: 8 (over z, y).
Axes of the slice: x: 2, y: 2, z: 4, core: 2. Of those that a mesh axis runs over, the one named last changes fastest.
Arguments:
- tokens: bfloat16 [4, 256, 3200], P('req', 'tp'), may hold values from -6 to 6
- segments: int32 [4, 256], P('req'), may hold values from -1 to 3, as said below
- norm_gain: float32 [3200], replicated, may hold values from 0.25 to 1.75
- wqkv: bfloat16 [3, 3200, 2048], P(None, None, 'tp'), may hold values from -4 to 4
- qk_gain: float32 [2, 2048], P(None, 'tp'), may hold values from 0.6 to 4
- wproj: bfloat16 [2048, 3200], P('tp'), may hold values from -0.125 to 0.125
- bproj: float32 [3200], P('tp'), may hold values from -3 to 3
- layer_scale: float32 [3200], P('tp'), may hold values from 0.3 to 1.5
- ln_weight: float32 [4, 3200], P(None, 'tp'), may hold values from 0.25 to 1.75
- ln_bias: float32 [4, 3200], P(None, 'tp'), may hold values from -2 to 2
- w_merge: bfloat16 [4, 3200, 3072], P(None, 'tp'), may hold values from -0.0546875 to 0.0546875
- b_merge: float32 [3072], replicated, may hold values from -3 to 3
- owners: int32 [4, 64, 1], P(None, 'tp'), may hold values from 0 to 3; in each aligned block of 8 rows (0 to 7, 8 to 15, ..., all dimensions but the last counted through in order) at most 3 rows name the same one
Outputs:
- lm_inputs: bfloat16 [4, 4, 8, 3, 3072], P('req', None, 'tp')
The draws below stay inside these ranges and needn't reach their ends.
Inputs may be any that keep to these rules, and one draw needn't show every extreme that they name: `segments`: each group's tokens are whole images, each a whole number of blocks of 64 tokens (two patch rows); image numbers start at 0 and never fall; padding tokens (-1) fill the end of a group from a block boundary; some group has no padding and some group has padding. `owners`: among the 8 merged tokens of one device (aligned blocks of one group), at most 3 name the same owner.
All inputs are finite; a program needn't handle non-finite values.
Results may differ from the reference program's by a relative error of at most 0.014.
Values may be sent and summed in bfloat16 or wider, within the bound.
A program may use at most 64 MiB of HBM per device.

```python
import math
import jax
import jax.numpy as jnp
import numpy as np
from jax import lax

D = 3200
HEADS = 16
HD = 128
PF = 3072
PW = 32
TOK = 256
MERGED = 64
MD = 8
CAP = 3
N_REQ = 4
N_TP = 8


def draw_segments(key, part):
    pair_count = TOK // (2 * PW)
    subkeys = jax.random.split(key, 3)
    full_group = jax.random.randint(subkeys[2], (), 0, N_REQ)
    padded_group = (full_group + 1) % N_REQ
    group_ids = jnp.arange(N_REQ)
    image_cuts = (jax.random.randint(subkeys[0], (N_REQ, pair_count), 0, 3) == 0).astype(jnp.int32)
    image_cuts = jnp.where((group_ids == full_group)[:, None], 1, image_cuts)
    image_cuts = image_cuts.at[:, 0].set(0)
    pair_ids = jnp.cumsum(image_cuts, axis=1)
    kept_pairs = jax.random.randint(subkeys[1], (N_REQ,), (pair_count + 1) // 2, pair_count + 1)
    kept_pairs = jnp.where(group_ids == padded_group, jnp.minimum(kept_pairs, pair_count - 1), kept_pairs)
    kept_pairs = jnp.where(group_ids == full_group, pair_count, kept_pairs)
    live_pairs = jnp.arange(pair_count)[None, :] < kept_pairs[:, None]
    pair_ids = jnp.where(live_pairs, pair_ids, -1)
    return jnp.repeat(pair_ids, 2 * PW, axis=1).astype(jnp.int32)


def draw_wqkv(key, part):
    inner_width = HEADS * HD
    subkeys = jax.random.split(key, 2)
    head_rank = (jnp.arange(inner_width) // HD).astype(jnp.float32)
    rising = jnp.exp(jnp.log(3.0) * head_rank / float(HEADS - 1))
    column_scale = jax.random.uniform(subkeys[1], (3, 1, inner_width), jnp.float32, 0.6, 1.4)
    base_draw = jax.random.normal(subkeys[0], (3, D, inner_width), jnp.float32)
    return (base_draw * column_scale * rising[None, None, :] * D ** (-0.5)).astype(jnp.bfloat16)


def draw_qk_gain(key, part):
    return jax.random.uniform(key, (2, HEADS * HD), jnp.float32, 0.6, 1.4)


def block_levels(key, extent, pieces, smallest, high):
    gain = 1.0
    for axis_at, parts in pieces:
        heights = jax.random.uniform(jax.random.fold_in(jax.random.fold_in(key, 6), axis_at), (parts,), jnp.float32, smallest / len(pieces), high / len(pieces))
        gain = gain * jnp.repeat(jnp.exp(heights), extent[axis_at] // parts).reshape((-1,) + (1,) * (len(extent) - 1 - axis_at))
    return gain


def deal_out(stream_key, own, number, rows, count, top, bound, skew):
    sequence = jax.random.permutation(stream_key, count)
    packed, common = shares(count, rows * top, bound, skew, True), shares(count, rows * top, bound, skew, False)
    places = jnp.arange(count)

    def named(tallies, rotation):
        used = int((tallies > 0).sum())
        fixed = max(1, used // 4)
        passed = fixed + (places - fixed + rotation * (used - fixed)) % max(1, count - fixed)
        return jnp.zeros((count,), jnp.int32).at[sequence[jnp.where(places < fixed, places, passed)]].set(jnp.asarray(tallies, jnp.int32))

    tallies = jnp.where(number % 4 == 0, named(packed, number // 4), named(common, number - number // 4 - 1))
    mixed = jax.random.permutation(jax.random.fold_in(own, 3), count)
    giver, sink = mixed[0:count // 2 * 2:2], mixed[1:count // 2 * 2:2]
    room = jnp.minimum(tallies[giver] - 1, bound - tallies[sink]) // 2
    room = jnp.where((giver == sequence[0]) | (sink == sequence[0]) | (tallies[sink] == 0), 0, jnp.maximum(room, 0))
    passed = jax.random.randint(jax.random.fold_in(own, 4), (count // 2,), 0, 1 << 20) % (room + 1)
    tallies = tallies.at[giver].add(-passed).at[sink].add(passed)
    items = jnp.searchsorted(jnp.cumsum(tallies), jnp.arange(rows * top), side="right").astype(jnp.int32)
    grid = items.reshape(top, rows).T
    grid = grid[jax.random.permutation(jax.random.fold_in(own, 1), rows)]
    rotation = jax.random.randint(jax.random.fold_in(own, 2), (rows, 1), 0, top)
    return jnp.take_along_axis(grid, (jnp.arange(top)[None, :] + rotation) % top, axis=1)


def shares(number_of, total, reach, skew, full):
    portions = [(1 << 20) // math.isqrt(rank ** skew) + 1 for rank in range(1, number_of + 1)]
    largest = reach if full else min(reach, max(-(-total // number_of), total * portions[0] // sum(portions)))
    least = 1 if total - largest >= number_of - 1 else 0
    given, spare = [largest] + [least] * (number_of - 1), total - largest - least * (number_of - 1)
    while spare > 0:
        candidates = [i for i in range(1, number_of) if given[i] < largest] or [i for i in range(1, number_of) if given[i] < reach]
        whole, budget = sum([portions[i] for i in candidates]), spare
        for i in candidates:
            more = min(reach - given[i], max(1, budget * portions[i] // whole), spare)
            given[i] = given[i] + more
            spare = spare - more
    return np.array(given)


def centred(key, extent, deviation, limit, cuts=(), kind=jnp.bfloat16):
    gain = block_levels(key, extent, cuts, -0.22, 0.18) if cuts else 1.0
    drawn = jax.random.normal(key, extent, jnp.float32) * deviation * gain
    return jnp.minimum(jnp.maximum(drawn, -limit), limit).astype(kind)


def setup_inputs(seed: int = 0) -> dict:
    arg_keys = jax.random.split(jax.random.key(seed), 14)
    tokens = centred(arg_keys[0], (N_REQ, TOK, D), 1.0, 6.0, ((0, 4), (1, 8)))
    segments = draw_segments(jax.random.fold_in(arg_keys[13], 71), 0)
    norm_gain = jnp.clip(1.0 + 0.15 * jax.random.normal(arg_keys[2], (D,), jnp.float32), 0.25, 1.75)
    wqkv = draw_wqkv(jax.random.fold_in(arg_keys[13], 71), 0)
    qk_gain = draw_qk_gain(jax.random.fold_in(arg_keys[13], 71), 0)
    wproj = centred(arg_keys[5], (HEADS * HD, D), (HEADS * HD) ** -0.5, 0.125, ((0, 8),))
    bproj = centred(arg_keys[6], (D,), 0.5, 3.0, ((0, 8),), jnp.float32)
    layer_scale = jnp.clip(jnp.exp(math.log(1.5) - 1.60943787 * jax.random.uniform(arg_keys[7], (D,), jnp.float32) ** block_levels(arg_keys[7], (D,), ((0, 8),), -0.2, 0.2)), 0.3, 1.5)
    ln_weight = jnp.clip(1.0 + 0.15 * jax.random.normal(arg_keys[8], (4, D), jnp.float32), 0.25, 1.75)
    ln_bias = centred(arg_keys[9], (4, D), 0.3, 2.0, ((1, 8),), jnp.float32)
    w_merge = centred(arg_keys[10], (4, D, PF), (4 * D) ** -0.5, 0.0546875, ((1, 8),))
    b_merge = centred(arg_keys[11], (PF,), 0.5, 3.0, (), jnp.float32)
    owners_keys = jax.random.split(jax.random.fold_in(arg_keys[12], 1), N_REQ * MERGED // MD)
    owners_turns = jax.random.permutation(jax.random.fold_in(arg_keys[12], 3), N_REQ * MERGED // MD)
    owners = jax.vmap(lambda own, number: deal_out(jax.random.fold_in(arg_keys[12], 2), own, number, MD, N_REQ, 1, CAP, 2))(owners_keys, owners_turns).reshape((N_REQ, MERGED, 1))
    return dict(tokens=tokens, segments=segments, norm_gain=norm_gain, wqkv=wqkv, qk_gain=qk_gain, wproj=wproj, bproj=bproj, layer_scale=layer_scale, ln_weight=ln_weight, ln_bias=ln_bias, w_merge=w_merge, b_merge=b_merge, owners=owners)


EPS_RMS = 1e-06
EPS_LN = 1e-05

def block_count(length):
    number = max(1, length // 512)
    while length % number:
        number = number - 1
    return number

def attend_block(query_rows, key_heads, value_heads, query_segs, key_segs):
    scores = jnp.einsum('hqd,hkd->hqk', query_rows.astype(jnp.float32), key_heads.astype(jnp.float32)) * HD ** (-0.5)
    same_image = query_segs[:, None] == key_segs[None, :]
    scores = jnp.where(same_image[None], scores, -jnp.inf)
    row_max = lax.optimization_barrier(jnp.max(scores, axis=-1, keepdims=True))
    weights = jnp.exp(scores - row_max)
    probabilities = (weights / lax.optimization_barrier(jnp.sum(weights, axis=-1, keepdims=True))).astype(jnp.bfloat16)
    mixed = jnp.einsum('hqk,hkd->hqd', probabilities.astype(jnp.float32), value_heads.astype(jnp.float32))
    return mixed.astype(jnp.bfloat16)

def merge_rows(stream):
    feature_count = stream.shape[-1]
    shaped = stream.reshape(stream.shape[0] // (2 * PW), 2, PW // 2, 2, feature_count)
    return shaped.transpose(0, 2, 1, 3, 4).reshape(stream.shape[0] // 4, 4, feature_count)

def reference(tokens, segments, norm_gain, wqkv, qk_gain, wproj, bproj, layer_scale, ln_weight, ln_bias, w_merge, b_merge, owners):
    inner_width = HEADS * HD

    def encode_group(group_item):
        group_tokens, group_segs = group_item
        widened = group_tokens.astype(jnp.float32)
        normed = (widened * lax.rsqrt(lax.optimization_barrier(jnp.mean(widened * widened, axis=-1, keepdims=True)) + EPS_RMS) * norm_gain).astype(jnp.bfloat16)
        q_part = jnp.dot(normed, wqkv[0], preferred_element_type=jnp.float32)
        k_part = jnp.dot(normed, wqkv[1], preferred_element_type=jnp.float32)
        v_part = jnp.dot(normed, wqkv[2], preferred_element_type=jnp.float32)
        q_scaled = (q_part * lax.rsqrt(lax.optimization_barrier(jnp.mean(q_part * q_part, axis=-1, keepdims=True)) + EPS_RMS) * qk_gain[0]).astype(jnp.bfloat16)
        k_scaled = (k_part * lax.rsqrt(lax.optimization_barrier(jnp.mean(k_part * k_part, axis=-1, keepdims=True)) + EPS_RMS) * qk_gain[1]).astype(jnp.bfloat16)
        v_scaled = v_part.astype(jnp.bfloat16)

        def split_heads(matrix):
            return matrix.reshape(TOK, HEADS, HD).transpose(1, 0, 2)
        block_total = block_count(TOK)
        block_rows = TOK // block_total
        query_blocks = split_heads(q_scaled).reshape(HEADS, block_total, block_rows, HD).transpose(1, 0, 2, 3)
        seg_blocks = group_segs.reshape(block_total, block_rows)
        key_heads = split_heads(k_scaled)
        value_heads = split_heads(v_scaled)
        mixed = lax.map(lambda block_item: attend_block(block_item[0], key_heads, value_heads, block_item[1], group_segs), (query_blocks, seg_blocks))
        attended = mixed.transpose(0, 2, 1, 3).reshape(TOK, inner_width)
        attn_out = jnp.dot(attended, wproj, preferred_element_type=jnp.float32)
        stream = (widened + layer_scale * (attn_out + bproj)).astype(jnp.bfloat16)
        merged = merge_rows(stream).reshape(MERGED, 4 * D).astype(jnp.float32)
        row_mean = lax.optimization_barrier(jnp.mean(merged, axis=-1, keepdims=True))
        centered = merged - row_mean
        row_var = lax.optimization_barrier(jnp.mean(centered * centered, axis=-1, keepdims=True))
        normal_rows = (centered * lax.rsqrt(row_var + EPS_LN) * ln_weight.reshape(4 * D) + ln_bias.reshape(4 * D)).astype(jnp.bfloat16)
        lifted = jnp.dot(normal_rows, w_merge.reshape(4 * D, PF), preferred_element_type=jnp.float32) + b_merge
        first_tokens = merge_rows(group_segs.reshape(TOK, 1))[:, 0, 0]
        live_rows = (first_tokens >= 0).astype(jnp.float32)
        return (jax.nn.gelu(lifted, approximate=False) * live_rows[:, None]).astype(jnp.bfloat16)
    projected = lax.map(encode_group, (tokens, segments))
    owner_ids = owners[:, :, 0].reshape(N_REQ, N_TP, MD)
    group_ids = jnp.arange(N_REQ, dtype=jnp.int32)
    owner_hits = (owner_ids[..., None] == group_ids).astype(jnp.int32)
    before = jnp.cumsum(owner_hits, axis=2) - owner_hits
    slot_rank = lax.optimization_barrier(jnp.sum(before * owner_hits, axis=-1))
    slot_ids = jnp.arange(CAP, dtype=jnp.int32)
    selector = (owner_ids[None, :, :, None, :] == group_ids[:, None, None, None, None]) & (slot_rank[None, :, :, None, :] == slot_ids[None, None, None, :, None])
    lm_inputs = jnp.einsum('dstcm,stmf->dstcf', selector.astype(jnp.float32), projected.reshape(N_REQ, N_TP, MD, PF).astype(jnp.float32))
    return lm_inputs.astype(jnp.bfloat16)
```

```python
import functools

import jax
import jax.numpy as jnp
from jax import lax
from jax.experimental import pallas as pl
from jax.experimental.pallas import tpu as pltpu
from jax.sharding import PartitionSpec as P

HD = 128
PW = 32
EPS_RMS = 1e-06
EPS_LN = 1e-05
MESH = pl.DeviceIdType.MESH
F32 = jnp.float32
BF16 = jnp.bfloat16


def dot_nt(left, right):
    return lax.dot_general(left, right, (((1,), (1,)), ((), ())), preferred_element_type=F32)


def iota(shape, axis):
    return lax.broadcasted_iota(jnp.int32, shape, axis)


def lanes_to_column(row, count):
    return jnp.transpose(jnp.broadcast_to(row, (128, count)))


def columns_to_lanes(first, second, rows):
    lane = iota((rows, 128), 1)
    both = jnp.where(lane == 0, first, jnp.where(lane == 1, second, 0.0))
    if rows < 128:
        both = jnp.concatenate([both, jnp.zeros((128 - rows, 128), F32)], axis=0)
    return jnp.transpose(both)[:8]


def rows_to_columns(first, second, count):
    row = iota((128, count), 0)
    return jnp.transpose(jnp.where(row == 0, first, jnp.where(row == 1, second, 0.0)))


def body(
    dims,
    tok, segs, gain, qk_gain, cols, ln_w, ln_b, bm, own_ref, wqkv_h, wproj_h, wm_h,
    out,
    wqkv, wproj, wm, gathered, normed, qkv, attended,
    sb1, rb1, sb2, rb2, acc, sumbox, sumsend, statbox, statsend,
    normal, sb3, rb3, live, ob, rbo,
    wsem, ag1_s, ag2_s, ag_r, sum_s, sum_r, rs1_s, rs1_r, rs2_s, rs2_r,
    st_s, st_r, m_s, m_r, o_s, o_r,
):
    A, B, T, R, G, E, EP, S, D, M, PF, CH = dims
    me = lax.axis_index("tp")
    grp = lax.axis_index("req")
    a, b = me // B, lax.rem(me, B)
    F = wqkv.shape[2]
    MD = M // T
    W = PF // CH // 2

    wcopies = [
        pltpu.make_async_copy(wqkv_h, wqkv, wsem.at[0]),
        pltpu.make_async_copy(wproj_h, wproj, wsem.at[1]),
        pltpu.make_async_copy(wm_h, wm, wsem.at[2]),
    ]
    for copy in wcopies:
        copy.start()

    barrier = pltpu.get_barrier_semaphore()
    for i in range(1, T):
        pl.semaphore_signal(barrier, inc=1, device_id={"tp": lax.rem(me + i, T)}, device_id_type=MESH)
    for i in range(1, G):
        pl.semaphore_signal(barrier, inc=1, device_id={"req": lax.rem(grp + i, G)}, device_id_type=MESH)
    pl.semaphore_wait(barrier, T - 1 + G - 1)

    def to_tp(src, dst, s, r, peer):
        return pltpu.make_async_remote_copy(
            src_ref=src, dst_ref=dst, send_sem=s, recv_sem=r,
            device_id={"tp": peer}, device_id_type=MESH,
        )

    sends = []

    def send(copy):
        copy.start()
        sends.append(copy)

    for i in range(1, A):
        send(to_tp(tok, gathered.at[me], ag1_s.at[i - 1], ag_r.at[me], lax.rem(a + i, A) * B + b))
    for j in range(1, B):
        send(to_tp(tok, gathered.at[me], ag2_s.at[j - 1], ag_r.at[me], a * B + lax.rem(b + j, B)))
    gathered[me] = tok[...]

    def arrived(slot):
        to_tp(gathered.at[slot], gathered.at[slot], ag1_s.at[0], ag_r.at[slot], me).wait_recv()

    def normalise(slot):
        x = gathered[slot].astype(F32)
        scale = lax.rsqrt(jnp.mean(x * x, axis=-1, keepdims=True) + EPS_RMS)
        normed[slot] = (x * scale * gain[...]).astype(BF16)

    def project(slots):
        rows = jnp.concatenate([normed[s] for s in slots], axis=0)
        for i in range(3):
            part = jnp.dot(rows, wqkv[i], preferred_element_type=F32)
            for n, s in enumerate(slots):
                qkv[i, s] = part[n * R:(n + 1) * R]

    seg_row = segs[...].astype(F32)
    seg_col = lanes_to_column(seg_row, S)
    token = iota((M, S), 1)
    merged_id = iota((M, S), 0)
    half = PW // 2
    base = 2 * PW * (merged_id // half) + 2 * lax.rem(merged_id, half)
    live[...] = jnp.dot(
        (token == base).astype(BF16), (seg_col >= 0).astype(BF16), preferred_element_type=F32
    )

    normalise(me)
    for i in range(1, A):
        slot = lax.rem(a + A - i, A) * B + b
        arrived(slot)
        for j in range(1, B):
            send(to_tp(
                gathered.at[slot], gathered.at[slot], ag2_s.at[i * (B - 1) + j - 1],
                ag_r.at[slot], a * B + lax.rem(b + j, B),
            ))
        normalise(slot)
    wcopies[0].wait()
    project([lax.rem(a + A - i, A) * B + b for i in range(A)])
    for j in range(1, B):
        slots = [lax.rem(a + A - i, A) * B + lax.rem(b + B - j, B) for i in range(A)]
        for slot in slots:
            arrived(slot)
            normalise(slot)
        project(slots)

    q_part = qkv[0].reshape(S, F)
    k_part = qkv[1].reshape(S, F)
    sumsend[...] = columns_to_lanes(
        jnp.sum(q_part * q_part, axis=-1, keepdims=True),
        jnp.sum(k_part * k_part, axis=-1, keepdims=True), S,
    )
    for i in range(1, T):
        send(to_tp(sumsend, sumbox.at[me], sum_s.at[i - 1], sum_r.at[me], lax.rem(me + i, T)))
    sumbox[me] = sumsend[...]
    for i in range(1, T):
        slot = lax.rem(me + i, T)
        to_tp(sumsend, sumbox.at[slot], sum_s.at[0], sum_r.at[slot], me).wait_recv()
    total = jnp.sum(sumbox[...], axis=0)
    inner = F * T
    scales = lax.rsqrt(total / inner + EPS_RMS)
    columns = rows_to_columns(scales[0:1], scales[1:2], S)
    q_all = (qkv[0].reshape(S, F) * columns[:, 0:1] * qk_gain[0:1, :]).astype(BF16)
    k_all = (qkv[1].reshape(S, F) * columns[:, 1:2] * qk_gain[1:2, :]).astype(BF16)
    v_all = qkv[2].reshape(S, F).astype(BF16)
    same = lanes_to_column(seg_row, S)[:, 0:1] == seg_row
    for h in range(F // HD):
        lo, hi = h * HD, (h + 1) * HD
        scores = jnp.where(same, dot_nt(q_all[:, lo:hi], k_all[:, lo:hi]) * HD ** (-0.5), -jnp.inf)
        weights = jnp.exp(scores - jnp.max(scores, axis=-1, keepdims=True))
        probabilities = (weights / jnp.sum(weights, axis=-1, keepdims=True)).astype(BF16)
        attended[:, lo:hi] = jnp.dot(
            probabilities, v_all[:, lo:hi], preferred_element_type=F32
        ).astype(BF16)

    wcopies[1].wait()
    for i in list(range(1, A)) + [0]:
        for j in range(1, B):
            dest_a, dest_b = lax.rem(a + i, A), lax.rem(b + j, B)
            sb1[j - 1, i] = dot_nt(wproj[dest_a * B + dest_b], attended[...]).astype(BF16)
            send(to_tp(sb1.at[j - 1, i], rb1.at[j - 1, i], rs1_s.at[j - 1, i],
                       rs1_r.at[j - 1, i], a * B + dest_b))
    for i in list(range(1, A)) + [0]:
        dest_a = lax.rem(a + i, A)
        part = dot_nt(wproj[dest_a * B + b], attended[...])
        for j in range(1, B):
            to_tp(sb1.at[j - 1, i], rb1.at[j - 1, i], rs1_s.at[j - 1, i],
                  rs1_r.at[j - 1, i], me).wait_recv()
            part = part + rb1[j - 1, i].astype(F32)
        if i:
            sb2[i - 1] = part.astype(BF16)
            send(to_tp(sb2.at[i - 1], rb2.at[i - 1], rs2_s.at[i - 1], rs2_r.at[i - 1],
                       dest_a * B + b))
        else:
            acc[...] = part
    KC = D // 5
    own = jnp.zeros((EP, S), F32)
    for c in range(5):
        pick = (iota((EP, KC), 1) + c * KC == iota((EP, KC), 0) + me * E).astype(BF16)
        own = own + dot_nt(pick, gathered[:, :, c * KC:(c + 1) * KC].reshape(S, KC))
    for i in range(1, A):
        to_tp(sb2.at[i - 1], rb2.at[i - 1], rs2_s.at[i - 1], rs2_r.at[i - 1], me).wait_recv()
    attn = acc[...]
    for i in range(1, A):
        attn = attn + rb2[i - 1].astype(F32)
    stream = (own + cols[:, 1:2] * (attn + cols[:, 0:1])).astype(BF16)

    merged = []
    for off in (0, 1, PW, PW + 1):
        merged.append(dot_nt((token == base + off).astype(BF16), stream)[:, :E])
    local = sum(jnp.sum(m, axis=-1, keepdims=True) for m in merged)
    local_mean = local / (4 * E)
    spread = sum(jnp.sum((m - local_mean) * (m - local_mean), axis=-1, keepdims=True) for m in merged)
    statsend[...] = columns_to_lanes(local, spread, M)
    for i in range(1, T):
        send(to_tp(statsend, statbox.at[me], st_s.at[i - 1], st_r.at[me], lax.rem(me + i, T)))
    statbox[me] = statsend[...]
    for i in range(1, T):
        slot = lax.rem(me + i, T)
        to_tp(statsend, statbox.at[slot], st_s.at[0], st_r.at[slot], me).wait_recv()
    stats = [statbox[t] for t in range(T)]
    mean_row = sum(s[0:1] for s in stats) / (4 * D)
    square_row = sum(s[1:2] for s in stats) + (4 * E) * sum(
        (s[0:1] / (4 * E) - mean_row) * (s[0:1] / (4 * E) - mean_row) for s in stats
    )
    stat_cols = rows_to_columns(mean_row, lax.rsqrt(square_row / (4 * D) + EPS_LN), 128)[:M]
    row_mean, row_scale = stat_cols[:, 0:1], stat_cols[:, 1:2]
    for n in range(4):
        normal[n] = (
            (merged[n] - row_mean) * row_scale * ln_w[n:n + 1, :] + ln_b[n:n + 1, :]
        ).astype(BF16)

    wcopies[2].wait()
    for c in range(CH):
        lo = 2 * W * c
        part = sum(
            jnp.dot(normal[n], wm[n, :, lo:lo + 2 * W], preferred_element_type=F32)
            for n in range(4)
        )
        for k in range(T):
            rows = part[k * MD:(k + 1) * MD]
            sb3[c, k] = jnp.concatenate([rows[:, :W], rows[:, W:]], axis=0).astype(BF16)
        rb3[c, me] = sb3[c, me]
        for i in range(1, T):
            peer = lax.rem(me + i, T)
            send(to_tp(sb3.at[c, peer], rb3.at[c, me], m_s.at[c, i - 1], m_r.at[c, me], peer))

    ids = jnp.broadcast_to(own_ref[grp].astype(F32), (MD, 128))
    ids_row = jnp.transpose(jnp.concatenate([ids] * (128 // MD), axis=0))
    lane = iota((MD, 128), 1)
    earlier = (ids == ids_row[:MD]) & (iota((MD, 128), 0) < lax.rem(lane, MD))
    rank = jnp.sum(earlier.astype(F32), axis=0, keepdims=True)
    N = 2 * CH
    rows = iota((G * 4 * N, 128), 0)
    lane = iota((G * 4 * N, 128), 1)
    pick = (
        (ids_row[0:1] == (rows // (4 * N)).astype(F32))
        & (rank == lax.rem(rows, 4).astype(F32))
        & (lane // MD == lax.rem(rows, 4 * N) // 4)
    )
    pick = pick.astype(BF16)[:, :N * MD]
    alive = live[pl.ds(pl.multiple_of(me * MD, MD), MD), :][:, 0:1]
    pieces = []
    for c in range(CH):
        for i in range(1, T):
            slot = lax.rem(me + i, T)
            to_tp(sb3.at[c, slot], rb3.at[c, slot], m_s.at[c, 0], m_r.at[c, slot], me).wait_recv()
        total = rb3[c, 0].astype(F32)
        for k in range(1, T):
            total = total + rb3[c, k].astype(F32)
        for h in range(2):
            at = (2 * c + h) * W
            x = total[h * MD:(h + 1) * MD] + bm[:, at:at + W]
            pieces.append(0.5 * x * (1.0 + lax.erf(x * (0.5 ** 0.5))) * alive)
    stacked = jnp.concatenate(pieces, axis=0).astype(BF16)
    ob[...] = jnp.dot(pick, stacked, preferred_element_type=F32).reshape(G, 4 * N, W).astype(BF16)
    for i in range(1, G):
        peer = lax.rem(grp + i, G)
        copy = pltpu.make_async_remote_copy(
            src_ref=ob.at[peer], dst_ref=rbo.at[grp], send_sem=o_s.at[i - 1],
            recv_sem=o_r.at[grp], device_id={"req": peer}, device_id_type=MESH,
        )
        copy.start()
        sends.append(copy)
    out[grp] = ob[grp]
    for i in range(1, G):
        slot = lax.rem(grp + i, G)
        pltpu.make_async_remote_copy(
            src_ref=ob.at[slot], dst_ref=rbo.at[slot], send_sem=o_s.at[0],
            recv_sem=o_r.at[slot], device_id={"req": grp}, device_id_type=MESH,
        ).wait_recv()
        out[slot] = rbo[slot]
    for copy in sends:
        copy.wait_send()


def per_device(
    tokens, segments, norm_gain, wqkv, qk_gain, wproj, bproj, layer_scale,
    ln_weight, ln_bias, w_merge, b_merge, owners,
):
    T = lax.axis_size("tp")
    G = lax.axis_size("req")
    A = 4
    B = T // A
    R, D = tokens.shape[1:]
    S = R * T
    F = wqkv.shape[2]
    E = bproj.shape[0]
    EP = -(-E // 16) * 16
    M = S // 4
    MD = M // T
    PF = w_merge.shape[2]
    CH = 2
    W = PF // CH // 2
    capacity = (MD + G - 1) // G + 1
    wproj_t = wproj.T.reshape(T, E, F)
    cols = jnp.stack([bproj, layer_scale], axis=1)
    if EP != E:
        wproj_t = jnp.pad(wproj_t, ((0, 0), (0, EP - E), (0, 0)))
        cols = jnp.pad(cols, ((0, EP - E), (0, 0)))
    dims = (A, B, T, R, G, E, EP, S, D, M, PF, CH)
    vmem = pl.BlockSpec(memory_space=pltpu.VMEM)
    hbm = pl.BlockSpec(memory_space=pl.ANY)
    dma = pltpu.SemaphoreType.DMA
    out = pl.pallas_call(
        functools.partial(body, dims),
        out_shape=jax.ShapeDtypeStruct((G, 8 * CH, W), BF16),
        in_specs=[vmem] * 9 + [hbm] * 3,
        out_specs=vmem,
        scratch_shapes=[
            pltpu.VMEM((3, D, F), BF16),
            pltpu.VMEM((T, EP, F), BF16),
            pltpu.VMEM((4, E, PF), BF16),
            pltpu.VMEM((T, R, D), BF16),
            pltpu.VMEM((T, R, D), BF16),
            pltpu.VMEM((3, T, R, F), F32),
            pltpu.VMEM((S, F), BF16),
            pltpu.VMEM((B - 1, A, EP, S), BF16),
            pltpu.VMEM((B - 1, A, EP, S), BF16),
            pltpu.VMEM((A - 1, EP, S), BF16),
            pltpu.VMEM((A - 1, EP, S), BF16),
            pltpu.VMEM((EP, S), F32),
            pltpu.VMEM((T, 8, S), F32),
            pltpu.VMEM((8, S), F32),
            pltpu.VMEM((T, 8, 128), F32),
            pltpu.VMEM((8, 128), F32),
            pltpu.VMEM((4, M, E), BF16),
            pltpu.VMEM((CH, T, 2 * MD, W), BF16),
            pltpu.VMEM((CH, T, 2 * MD, W), BF16),
            pltpu.VMEM((M, 128), F32),
            pltpu.VMEM((G, 8 * CH, W), BF16),
            pltpu.VMEM((G, 8 * CH, W), BF16),
            dma((3,)),
            dma((A - 1,)), dma((A * (B - 1),)), dma((T,)),
            dma((T - 1,)), dma((T,)),
            dma((B - 1, A)), dma((B - 1, A)),
            dma((A - 1,)), dma((A - 1,)),
            dma((T - 1,)), dma((T,)),
            dma((CH, T - 1)), dma((CH, T)),
            dma((G - 1,)), dma((G,)),
        ],
        compiler_params=pltpu.CompilerParams(
            collective_id=0, has_side_effects=True, vmem_limit_bytes=56 * 1024 * 1024
        ),
    )(
        tokens[0], segments, norm_gain.reshape(1, D), qk_gain, cols, ln_weight, ln_bias,
        b_merge.reshape(1, PF), owners, wqkv, wproj_t, w_merge,
    )
    slots = out.reshape(G, 2 * CH, 4, W).transpose(0, 2, 1, 3).reshape(G, 4, PF)
    return slots[:, :capacity].reshape(1, G, 1, capacity, PF)


def solution(mesh):
    placed = (
        P("req", "tp", None),
        P("req", None),
        P(),
        P(None, None, "tp"),
        P(None, "tp"),
        P("tp", None),
        P("tp"),
        P("tp"),
        P(None, "tp"),
        P(None, "tp"),
        P(None, "tp", None),
        P(),
        P(None, "tp", None),
    )
    return jax.shard_map(
        per_device,
        mesh=mesh,
        in_specs=placed,
        out_specs=P("req", None, "tp", None, None),
        check_vma=False,
    )
```

```python
import functools

import jax
import jax.numpy as jnp
from jax import lax
from jax.experimental import pallas as pl
from jax.experimental.pallas import tpu as pltpu
from jax.sharding import PartitionSpec as P

HD = 128
PW = 32
EPS_RMS = 1e-06
EPS_LN = 1e-05
MESH = pl.DeviceIdType.MESH
F32 = jnp.float32
BF16 = jnp.bfloat16


def dot_nt(left, right):
    return lax.dot_general(left, right, (((1,), (1,)), ((), ())), preferred_element_type=F32)


def iota(shape, axis):
    return lax.broadcasted_iota(jnp.int32, shape, axis)


def lanes_to_column(row, count):
    return jnp.transpose(jnp.broadcast_to(row, (128, count)))


def columns_to_lanes(first, second, rows):
    lane = iota((rows, 128), 1)
    both = jnp.where(lane == 0, first, jnp.where(lane == 1, second, 0.0))
    if rows < 128:
        both = jnp.concatenate([both, jnp.zeros((128 - rows, 128), F32)], axis=0)
    return jnp.transpose(both)[:8]


def rows_to_columns(first, second, count):
    row = iota((128, count), 0)
    return jnp.transpose(jnp.where(row == 0, first, jnp.where(row == 1, second, 0.0)))


def body(
    dims,
    tok, segs, gain, qk_gain, bias, lscale, ln_w, ln_b, bm, own_ref, wqkv_h, wproj_h, wm_h,
    out,
    wqkv, wproj_v, wm, turned, wproj, cols, gathered, normed, qkv, attended,
    sb1, rb1, sb2, rb2, acc, sumbox, sumsend, statbox, statsend,
    normal, sb3, rb3, live, ob, rbo, raw,
    wsem, ag1_s, ag2_s, ag_r, sum_s, sum_r, rs1_s, rs1_r, rs2_s, rs2_r,
    st_s, st_r, m_s, m_r, o_s, o_r,
):
    A, B, T, R, G, E, EP, S, D, M, PF, CH = dims
    me = lax.axis_index("tp")
    grp = lax.axis_index("req")
    a, b = me // B, lax.rem(me, B)
    F = wqkv.shape[2]
    MD = M // T
    W = PF // CH // 2

    wcopies = [
        pltpu.make_async_copy(wqkv_h, wqkv, wsem.at[0]),
        pltpu.make_async_copy(wproj_h, wproj_v, wsem.at[1]),
        pltpu.make_async_copy(wm_h, wm, wsem.at[2]),
    ]
    for copy in wcopies:
        copy.start()

    barrier = pltpu.get_barrier_semaphore()
    for i in range(1, T):
        pl.semaphore_signal(barrier, inc=1, device_id={"tp": lax.rem(me + i, T)}, device_id_type=MESH)
    for i in range(1, G):
        pl.semaphore_signal(barrier, inc=1, device_id={"req": lax.rem(grp + i, G)}, device_id_type=MESH)
    pl.semaphore_wait(barrier, T - 1 + G - 1)

    def to_tp(src, dst, s, r, peer):
        return pltpu.make_async_remote_copy(
            src_ref=src, dst_ref=dst, send_sem=s, recv_sem=r,
            device_id={"tp": peer}, device_id_type=MESH,
        )

    sends = []

    def send(copy):
        copy.start()
        sends.append(copy)

    C = gathered.shape[1]
    for c in range(C):
        for j in range(1, B):
            send(to_tp(tok.at[c], gathered.at[me, c], ag2_s.at[c, j - 1], ag_r.at[me, c],
                       a * B + lax.rem(b + j, B)))
        for i in range(1, A):
            send(to_tp(tok.at[c], gathered.at[me, c], ag1_s.at[c, i - 1], ag_r.at[me, c],
                       lax.rem(a + i, A) * B + b))
    gathered[me] = tok[...]

    def arrived(slot, c):
        to_tp(gathered.at[slot, c], gathered.at[slot, c], ag1_s.at[0, 0], ag_r.at[slot, c],
              me).wait_recv()

    def normalise(slot):
        x = gathered[slot].reshape(R, D).astype(F32)
        scale = lax.rsqrt(jnp.mean(x * x, axis=-1, keepdims=True) + EPS_RMS)
        normed[slot] = (x * scale * gain[...].reshape(1, D)).astype(BF16)

    def project(slots):
        rows = jnp.concatenate([normed[s] for s in slots], axis=0)
        for i in range(3):
            part = jnp.dot(rows, wqkv[i], preferred_element_type=F32)
            for n, s in enumerate(slots):
                qkv[i, s] = part[n * R:(n + 1) * R]

    seg_row = segs[...].astype(F32)
    seg_col = lanes_to_column(seg_row, S)
    token = iota((M, S), 1)
    merged_id = iota((M, S), 0)
    half = PW // 2
    base = 2 * PW * (merged_id // half) + 2 * lax.rem(merged_id, half)
    live[...] = jnp.dot(
        (token == base).astype(BF16), (seg_col >= 0).astype(BF16), preferred_element_type=F32
    )

    first = [lax.rem(a + A - i, A) * B + b for i in range(A)]
    for c in range(C):
        for i in range(1, A):
            slot = first[i]
            arrived(slot, c)
            for j in range(1, B):
                send(to_tp(
                    gathered.at[slot, c], gathered.at[slot, c],
                    ag2_s.at[c, i * (B - 1) + j - 1], ag_r.at[slot, c], a * B + lax.rem(b + j, B),
                ))
    for slot in first:
        normalise(slot)
    wcopies[0].wait()
    project(first)
    wcopies[1].wait()
    KC = D // 5
    for c in range(5):
        turned[c * KC:(c + 1) * KC, :] = jnp.transpose(
            wproj_v[:, c * KC:(c + 1) * KC].astype(F32)
        )
    for k in range(T):
        block = turned[k * E:(k + 1) * E, :]
        if EP != E:
            block = jnp.concatenate([block, jnp.zeros((EP - E, F), F32)], axis=0)
        wproj[k] = block.astype(BF16)
    row = iota((8, E), 0)
    two = jnp.where(row == 0, bias[...].reshape(1, E), jnp.where(row == 1, lscale[...].reshape(1, E), 0.0))
    cols[...] = lax.dot_general(
        (iota((EP, E), 0) == iota((EP, E), 1)).astype(F32), two, (((1,), (1,)), ((), ())),
        precision=lax.Precision.HIGHEST, preferred_element_type=F32,
    )
    for j in range(1, B):
        slots = [lax.rem(a + A - i, A) * B + lax.rem(b + B - j, B) for i in range(A)]
        for slot in slots:
            for c in range(C):
                arrived(slot, c)
            normalise(slot)
        project(slots)

    q_part = qkv[0].reshape(S, F)
    k_part = qkv[1].reshape(S, F)
    sumsend[...] = columns_to_lanes(
        jnp.sum(q_part * q_part, axis=-1, keepdims=True),
        jnp.sum(k_part * k_part, axis=-1, keepdims=True), S,
    )
    for i in range(1, T):
        send(to_tp(sumsend, sumbox.at[me], sum_s.at[i - 1], sum_r.at[me], lax.rem(me + i, T)))
    sumbox[me] = sumsend[...]
    q_all = (q_part * qk_gain[0:1, :]).astype(BF16)
    k_all = (k_part * qk_gain[1:2, :]).astype(BF16)
    v_all = qkv[2].reshape(S, F).astype(BF16)
    same = lanes_to_column(seg_row, S)[:, 0:1] == seg_row
    for h in range(F // HD):
        raw[h] = dot_nt(q_all[:, h * HD:(h + 1) * HD], k_all[:, h * HD:(h + 1) * HD])
    for i in range(1, T):
        slot = lax.rem(me + i, T)
        to_tp(sumsend, sumbox.at[slot], sum_s.at[0], sum_r.at[slot], me).wait_recv()
    total = jnp.sum(sumbox[...], axis=0)
    inner = F * T
    scales = lax.rsqrt(total / inner + EPS_RMS)
    query_scale = lanes_to_column(scales[0:1], S)[:, 0:1] * HD ** (-0.5)
    for h in range(F // HD):
        lo, hi = h * HD, (h + 1) * HD
        scores = jnp.where(same, raw[h] * query_scale * scales[1:2], -jnp.inf)
        weights = jnp.exp(scores - jnp.max(scores, axis=-1, keepdims=True))
        probabilities = (weights / jnp.sum(weights, axis=-1, keepdims=True)).astype(BF16)
        attended[:, lo:hi] = jnp.dot(
            probabilities, v_all[:, lo:hi], preferred_element_type=F32
        ).astype(BF16)

    for i in list(range(1, A)) + [0]:
        for j in range(1, B):
            dest_a, dest_b = lax.rem(a + i, A), lax.rem(b + j, B)
            sb1[j - 1, i] = dot_nt(wproj[dest_a * B + dest_b], attended[...]).astype(BF16)
            send(to_tp(sb1.at[j - 1, i], rb1.at[j - 1, i], rs1_s.at[j - 1, i],
                       rs1_r.at[j - 1, i], a * B + dest_b))
    for i in list(range(1, A)) + [0]:
        dest_a = lax.rem(a + i, A)
        part = dot_nt(wproj[dest_a * B + b], attended[...])
        for j in range(1, B):
            to_tp(sb1.at[j - 1, i], rb1.at[j - 1, i], rs1_s.at[j - 1, i],
                  rs1_r.at[j - 1, i], me).wait_recv()
            part = part + rb1[j - 1, i].astype(F32)
        if i:
            sb2[i - 1] = part.astype(BF16)
            send(to_tp(sb2.at[i - 1], rb2.at[i - 1], rs2_s.at[i - 1], rs2_r.at[i - 1],
                       dest_a * B + b))
        else:
            acc[...] = part
    own = jnp.zeros((EP, S), F32)
    for c in range(5):
        pick = (iota((EP, KC), 1) + c * KC == iota((EP, KC), 0) + me * E).astype(BF16)
        own = own + dot_nt(pick, gathered[:, :, :, c * KC:(c + 1) * KC].reshape(S, KC))
    for i in range(1, A):
        to_tp(sb2.at[i - 1], rb2.at[i - 1], rs2_s.at[i - 1], rs2_r.at[i - 1], me).wait_recv()
    attn = acc[...]
    for i in range(1, A):
        attn = attn + rb2[i - 1].astype(F32)
    stream = (own + cols[:, 1:2] * (attn + cols[:, 0:1])).astype(BF16)

    merged = []
    for off in (0, 1, PW, PW + 1):
        merged.append(dot_nt((token == base + off).astype(BF16), stream)[:, :E])
    local = sum(jnp.sum(m, axis=-1, keepdims=True) for m in merged)
    local_mean = local / (4 * E)
    spread = sum(jnp.sum((m - local_mean) * (m - local_mean), axis=-1, keepdims=True) for m in merged)
    statsend[...] = columns_to_lanes(local, spread, M)
    for i in range(1, T):
        send(to_tp(statsend, statbox.at[me], st_s.at[i - 1], st_r.at[me], lax.rem(me + i, T)))
    statbox[me] = statsend[...]
    for i in range(1, T):
        slot = lax.rem(me + i, T)
        to_tp(statsend, statbox.at[slot], st_s.at[0], st_r.at[slot], me).wait_recv()
    stats = [statbox[t] for t in range(T)]
    mean_row = sum(s[0:1] for s in stats) / (4 * D)
    square_row = sum(s[1:2] for s in stats) + (4 * E) * sum(
        (s[0:1] / (4 * E) - mean_row) * (s[0:1] / (4 * E) - mean_row) for s in stats
    )
    stat_cols = rows_to_columns(mean_row, lax.rsqrt(square_row / (4 * D) + EPS_LN), 128)[:M]
    row_mean, row_scale = stat_cols[:, 0:1], stat_cols[:, 1:2]
    for n in range(4):
        normal[n] = (
            (merged[n] - row_mean) * row_scale * ln_w[n:n + 1, :] + ln_b[n:n + 1, :]
        ).astype(BF16)

    wcopies[2].wait()
    for c in range(CH):
        lo = 2 * W * c
        part = sum(
            jnp.dot(normal[n], wm[n, :, lo:lo + 2 * W], preferred_element_type=F32)
            for n in range(4)
        )
        for k in range(T):
            rows = part[k * MD:(k + 1) * MD]
            sb3[c, k] = jnp.concatenate([rows[:, :W], rows[:, W:]], axis=0).astype(BF16)
        rb3[c, me] = sb3[c, me]
        for i in range(1, T):
            peer = lax.rem(me + i, T)
            send(to_tp(sb3.at[c, peer], rb3.at[c, me], m_s.at[c, i - 1], m_r.at[c, me], peer))

    spot = (lax.rem(iota((MD, 128), 1), MD) == iota((MD, 128), 0)).astype(F32)
    ids_row = jnp.dot(
        jnp.broadcast_to(own_ref[pl.ds(grp, 1), :].astype(F32), (128, MD)), spot,
        preferred_element_type=F32,
    )
    ids = jnp.transpose(ids_row)[:MD]
    lane = iota((MD, 128), 1)
    earlier = (ids == ids_row[:MD]) & (iota((MD, 128), 0) < lax.rem(lane, MD))
    rank = jnp.sum(earlier.astype(F32), axis=0, keepdims=True)
    N = 2 * CH
    rows = iota((G * 4 * N, 128), 0)
    lane = iota((G * 4 * N, 128), 1)
    pick = (
        (ids_row[0:1] == (rows // (4 * N)).astype(F32))
        & (rank == lax.rem(rows, 4).astype(F32))
        & (lane // MD == lax.rem(rows, 4 * N) // 4)
    )
    pick = pick.astype(BF16)[:, :N * MD]
    alive = live[pl.ds(pl.multiple_of(me * MD, MD), MD), :][:, 0:1]
    pieces = []
    for c in range(CH):
        for i in range(1, T):
            slot = lax.rem(me + i, T)
            to_tp(sb3.at[c, slot], rb3.at[c, slot], m_s.at[c, 0], m_r.at[c, slot], me).wait_recv()
        total = rb3[c, 0].astype(F32)
        for k in range(1, T):
            total = total + rb3[c, k].astype(F32)
        for h in range(2):
            at = (2 * c + h) * W
            x = total[h * MD:(h + 1) * MD] + bm[at:at + W].reshape(1, W)
            pieces.append(0.5 * x * (1.0 + lax.erf(x * (0.5 ** 0.5))) * alive)
    stacked = jnp.concatenate(pieces, axis=0).astype(BF16)
    ob[...] = jnp.dot(pick, stacked, preferred_element_type=F32).reshape(G, 4 * N, W).astype(BF16)
    for i in range(1, G):
        peer = lax.rem(grp + i, G)
        copy = pltpu.make_async_remote_copy(
            src_ref=ob.at[peer], dst_ref=rbo.at[grp], send_sem=o_s.at[i - 1],
            recv_sem=o_r.at[grp], device_id={"req": peer}, device_id_type=MESH,
        )
        copy.start()
        sends.append(copy)
    out[grp] = ob[grp]
    for i in range(1, G):
        slot = lax.rem(grp + i, G)
        pltpu.make_async_remote_copy(
            src_ref=ob.at[slot], dst_ref=rbo.at[slot], send_sem=o_s.at[0],
            recv_sem=o_r.at[slot], device_id={"req": grp}, device_id_type=MESH,
        ).wait_recv()
        out[slot] = rbo[slot]
    for copy in sends:
        copy.wait_send()


def per_device(
    tokens, segments, norm_gain, wqkv, qk_gain, wproj, bproj, layer_scale,
    ln_weight, ln_bias, w_merge, b_merge, owners,
):
    T = lax.axis_size("tp")
    G = lax.axis_size("req")
    A = 4
    B = T // A
    R, D = tokens.shape[1:]
    S = R * T
    F = wqkv.shape[2]
    E = bproj.shape[0]
    EP = -(-E // 16) * 16
    M = S // 4
    MD = M // T
    PF = w_merge.shape[2]
    CH = 2
    W = PF // CH // 2
    capacity = (MD + G - 1) // G + 1
    C = 2
    dims = (A, B, T, R, G, E, EP, S, D, M, PF, CH)
    vmem = pl.BlockSpec(memory_space=pltpu.VMEM)
    hbm = pl.BlockSpec(memory_space=pl.ANY)
    dma = pltpu.SemaphoreType.DMA
    out = pl.pallas_call(
        functools.partial(body, dims),
        out_shape=jax.ShapeDtypeStruct((G, 8 * CH, W), BF16),
        in_specs=[vmem] * 10 + [hbm] * 3,
        out_specs=vmem,
        scratch_shapes=[
            pltpu.VMEM((3, D, F), BF16),
            pltpu.VMEM((F, D), BF16),
            pltpu.VMEM((4, E, PF), BF16),
            pltpu.VMEM((D, F), F32),
            pltpu.VMEM((T, EP, F), BF16),
            pltpu.VMEM((EP, 8), F32),
            pltpu.VMEM((T, C, R // C, D), BF16),
            pltpu.VMEM((T, R, D), BF16),
            pltpu.VMEM((3, T, R, F), F32),
            pltpu.VMEM((S, F), BF16),
            pltpu.VMEM((B - 1, A, EP, S), BF16),
            pltpu.VMEM((B - 1, A, EP, S), BF16),
            pltpu.VMEM((A - 1, EP, S), BF16),
            pltpu.VMEM((A - 1, EP, S), BF16),
            pltpu.VMEM((EP, S), F32),
            pltpu.VMEM((T, 8, S), F32),
            pltpu.VMEM((8, S), F32),
            pltpu.VMEM((T, 8, 128), F32),
            pltpu.VMEM((8, 128), F32),
            pltpu.VMEM((4, M, E), BF16),
            pltpu.VMEM((CH, T, 2 * MD, W), BF16),
            pltpu.VMEM((CH, T, 2 * MD, W), BF16),
            pltpu.VMEM((M, 128), F32),
            pltpu.VMEM((G, 8 * CH, W), BF16),
            pltpu.VMEM((G, 8 * CH, W), BF16),
            pltpu.VMEM((F // HD, S, S), F32),
            dma((3,)),
            dma((C, A - 1)), dma((C, A * (B - 1))), dma((T, C)),
            dma((T - 1,)), dma((T,)),
            dma((B - 1, A)), dma((B - 1, A)),
            dma((A - 1,)), dma((A - 1,)),
            dma((T - 1,)), dma((T,)),
            dma((CH, T - 1)), dma((CH, T)),
            dma((G - 1,)), dma((G,)),
        ],
        compiler_params=pltpu.CompilerParams(
            collective_id=0, has_side_effects=True, vmem_limit_bytes=56 * 1024 * 1024
        ),
    )(
        tokens.reshape(C, R // C, D), segments, norm_gain, qk_gain, bproj, layer_scale,
        ln_weight, ln_bias, b_merge, owners[:, :, 0], wqkv, wproj, w_merge,
    )
    slots = out.reshape(G, 2 * CH, 4, W).transpose(0, 2, 1, 3).reshape(G, 4, PF)
    return slots[:, :capacity].reshape(1, G, 1, capacity, PF)


def solution(mesh):
    placed = (
        P("req", "tp", None),
        P("req", None),
        P(),
        P(None, None, "tp"),
        P(None, "tp"),
        P("tp", None),
        P("tp"),
        P("tp"),
        P(None, "tp"),
        P(None, "tp"),
        P(None, "tp", None),
        P(),
        P(None, "tp", None),
    )
    return jax.shard_map(
        per_device,
        mesh=mesh,
        in_specs=placed,
        out_specs=P("req", None, "tp", None, None),
        check_vma=False,
    )
```

```python
import functools

import jax
import jax.numpy as jnp
from jax import lax
from jax.experimental import pallas as pl
from jax.experimental.pallas import tpu as pltpu
from jax.sharding import PartitionSpec as P

HD = 128
PW = 32
EPS_RMS = 1e-06
EPS_LN = 1e-05
MESH = pl.DeviceIdType.MESH
F32 = jnp.float32
BF16 = jnp.bfloat16


def dot_nt(left, right):
    return lax.dot_general(left, right, (((1,), (1,)), ((), ())), preferred_element_type=F32)


def iota(shape, axis):
    return lax.broadcasted_iota(jnp.int32, shape, axis)


def lanes_to_column(row, count):
    return jnp.transpose(jnp.broadcast_to(row, (128, count)))


def columns_to_lanes(first, second, rows):
    lane = iota((rows, 128), 1)
    both = jnp.where(lane == 0, first, jnp.where(lane == 1, second, 0.0))
    if rows < 128:
        both = jnp.concatenate([both, jnp.zeros((128 - rows, 128), F32)], axis=0)
    return jnp.transpose(both)[:8]


def rows_to_columns(first, second, count):
    row = iota((128, count), 0)
    return jnp.transpose(jnp.where(row == 0, first, jnp.where(row == 1, second, 0.0)))


def body(
    dims,
    tok, segs, gain, qk_gain, bias, lscale, ln_w, ln_b, bm, own_ref, wqkv_h, wproj_h, wm_h,
    out,
    wqkv, wproj_v, wm, turned, wproj, cols, gathered, normed, qkv, attended,
    sb1, rb1, sb2, rb2, acc, sumbox, sumsend, statbox, statsend,
    normal, sb3, rb3, live, ob, rbo, raw,
    wsem, ag1_s, ag2_s, ag_r, sum_s, sum_r, rs1_s, rs1_r, rs2_s, rs2_r,
    st_s, st_r, m_s, m_r, o_s, o_r,
):
    A, B, T, R, G, E, EP, S, D, M, PF, CH = dims
    me = lax.axis_index("tp")
    grp = lax.axis_index("req")
    a, b = me // B, lax.rem(me, B)
    F = wqkv.shape[2]
    MD = M // T
    W = PF // CH // 2

    wcopies = [
        pltpu.make_async_copy(wqkv_h, wqkv, wsem.at[0]),
        pltpu.make_async_copy(wproj_h, wproj_v, wsem.at[1]),
        pltpu.make_async_copy(wm_h, wm, wsem.at[2]),
    ]
    for copy in wcopies:
        copy.start()

    barrier = pltpu.get_barrier_semaphore()
    for i in range(1, T):
        pl.semaphore_signal(barrier, inc=1, device_id={"tp": lax.rem(me + i, T)}, device_id_type=MESH)
    for i in range(1, G):
        pl.semaphore_signal(barrier, inc=1, device_id={"req": lax.rem(grp + i, G)}, device_id_type=MESH)
    pl.semaphore_wait(barrier, T - 1 + G - 1)

    def to_tp(src, dst, s, r, peer):
        return pltpu.make_async_remote_copy(
            src_ref=src, dst_ref=dst, send_sem=s, recv_sem=r,
            device_id={"tp": peer}, device_id_type=MESH,
        )

    sends = []

    def send(copy):
        copy.start()
        sends.append(copy)

    C = gathered.shape[1]
    partners = [a, a + 1 - 2 * lax.rem(a, 2), lax.rem(a + 2, A), A - 1 - a]
    for c in range(C):
        for j in range(1, B):
            send(to_tp(tok.at[c], gathered.at[me, c], ag2_s.at[c, j - 1], ag_r.at[me, c],
                       a * B + lax.rem(b + j, B)))
        for i in range(1, A):
            send(to_tp(tok.at[c], gathered.at[me, c], ag1_s.at[c, i - 1], ag_r.at[me, c],
                       partners[i] * B + b))
    gathered[me] = tok[...]

    def arrived(slot, c):
        to_tp(gathered.at[slot, c], gathered.at[slot, c], ag1_s.at[0, 0], ag_r.at[slot, c],
              me).wait_recv()

    def normalise(slot):
        x = gathered[slot].reshape(R, D).astype(F32)
        scale = lax.rsqrt(jnp.mean(x * x, axis=-1, keepdims=True) + EPS_RMS)
        normed[slot] = (x * scale * gain[...].reshape(1, D)).astype(BF16)

    def project(slots, which=(0, 1, 2)):
        rows = jnp.concatenate([normed[s] for s in slots], axis=0)
        for i in which:
            part = jnp.dot(rows, wqkv[i], preferred_element_type=F32)
            for n, s in enumerate(slots):
                qkv[i, s] = part[n * R:(n + 1) * R]

    seg_row = segs[...].astype(F32)
    seg_col = lanes_to_column(seg_row, S)
    token = iota((M, S), 1)
    merged_id = iota((M, S), 0)
    half = PW // 2
    base = 2 * PW * (merged_id // half) + 2 * lax.rem(merged_id, half)
    live[...] = jnp.dot(
        (token == base).astype(BF16), (seg_col >= 0).astype(BF16), preferred_element_type=F32
    )

    first = [p * B + b for p in partners]
    for c in range(C):
        for i in range(1, A):
            slot = first[i]
            arrived(slot, c)
            for j in range(1, B):
                send(to_tp(
                    gathered.at[slot, c], gathered.at[slot, c],
                    ag2_s.at[c, i * (B - 1) + j - 1], ag_r.at[slot, c], a * B + lax.rem(b + j, B),
                ))
    for slot in first:
        normalise(slot)
    wcopies[0].wait()
    project(first)
    wcopies[1].wait()
    KC = D // 5
    for c in range(5):
        turned[c * KC:(c + 1) * KC, :] = jnp.transpose(
            wproj_v[:, c * KC:(c + 1) * KC].astype(F32)
        )
    for k in range(T):
        block = turned[k * E:(k + 1) * E, :]
        if EP != E:
            block = jnp.concatenate([block, jnp.zeros((EP - E, F), F32)], axis=0)
        wproj[k] = block.astype(BF16)
    row = iota((8, E), 0)
    two = jnp.where(row == 0, bias[...].reshape(1, E), jnp.where(row == 1, lscale[...].reshape(1, E), 0.0))
    cols[...] = lax.dot_general(
        (iota((EP, E), 0) == iota((EP, E), 1)).astype(F32), two, (((1,), (1,)), ((), ())),
        precision=lax.Precision.HIGHEST, preferred_element_type=F32,
    )
    for j in range(1, B):
        slots = [p * B + lax.rem(b + B - j, B) for p in partners]
        for slot in slots:
            for c in range(C):
                arrived(slot, c)
            normalise(slot)
        project(slots, (0, 1) if j == B - 1 else (0, 1, 2))

    q_part = qkv[0].reshape(S, F)
    k_part = qkv[1].reshape(S, F)
    sumsend[...] = columns_to_lanes(
        jnp.sum(q_part * q_part, axis=-1, keepdims=True),
        jnp.sum(k_part * k_part, axis=-1, keepdims=True), S,
    )
    for i in range(1, T):
        send(to_tp(sumsend, sumbox.at[me], sum_s.at[i - 1], sum_r.at[me], lax.rem(me + i, T)))
    sumbox[me] = sumsend[...]
    project(slots, (2,))
    q_all = (q_part * qk_gain[0:1, :]).astype(BF16)
    k_all = (k_part * qk_gain[1:2, :]).astype(BF16)
    v_all = qkv[2].reshape(S, F).astype(BF16)
    same = lanes_to_column(seg_row, S)[:, 0:1] == seg_row
    for h in range(F // HD):
        raw[h] = dot_nt(q_all[:, h * HD:(h + 1) * HD], k_all[:, h * HD:(h + 1) * HD])
    for i in range(1, T):
        slot = lax.rem(me + i, T)
        to_tp(sumsend, sumbox.at[slot], sum_s.at[0], sum_r.at[slot], me).wait_recv()
    total = jnp.sum(sumbox[...], axis=0)
    inner = F * T
    scales = lax.rsqrt(total / inner + EPS_RMS)
    query_scale = lanes_to_column(scales[0:1], S)[:, 0:1] * HD ** (-0.5)
    for h in range(F // HD):
        lo, hi = h * HD, (h + 1) * HD
        scores = jnp.where(same, raw[h] * query_scale * scales[1:2], -jnp.inf)
        weights = jnp.exp(scores - jnp.max(scores, axis=-1, keepdims=True))
        probabilities = (weights / jnp.sum(weights, axis=-1, keepdims=True)).astype(BF16)
        attended[:, lo:hi] = jnp.dot(
            probabilities, v_all[:, lo:hi], preferred_element_type=F32
        ).astype(BF16)

    for i in list(range(1, A)) + [0]:
        for j in range(1, B):
            dest_a, dest_b = lax.rem(a + i, A), lax.rem(b + j, B)
            sb1[j - 1, i] = dot_nt(wproj[dest_a * B + dest_b], attended[...]).astype(BF16)
            send(to_tp(sb1.at[j - 1, i], rb1.at[j - 1, i], rs1_s.at[j - 1, i],
                       rs1_r.at[j - 1, i], a * B + dest_b))
    for i in list(range(1, A)) + [0]:
        dest_a = lax.rem(a + i, A)
        part = dot_nt(wproj[dest_a * B + b], attended[...])
        for j in range(1, B):
            to_tp(sb1.at[j - 1, i], rb1.at[j - 1, i], rs1_s.at[j - 1, i],
                  rs1_r.at[j - 1, i], me).wait_recv()
            part = part + rb1[j - 1, i].astype(F32)
        if i:
            sb2[i - 1] = part.astype(BF16)
            send(to_tp(sb2.at[i - 1], rb2.at[i - 1], rs2_s.at[i - 1], rs2_r.at[i - 1],
                       dest_a * B + b))
        else:
            acc[...] = part
    own = jnp.zeros((EP, S), F32)
    for c in range(5):
        pick = (iota((EP, KC), 1) + c * KC == iota((EP, KC), 0) + me * E).astype(BF16)
        own = own + dot_nt(pick, gathered[:, :, :, c * KC:(c + 1) * KC].reshape(S, KC))
    for i in range(1, A):
        to_tp(sb2.at[i - 1], rb2.at[i - 1], rs2_s.at[i - 1], rs2_r.at[i - 1], me).wait_recv()
    attn = acc[...]
    for i in range(1, A):
        attn = attn + rb2[i - 1].astype(F32)
    stream = (own + cols[:, 1:2] * (attn + cols[:, 0:1])).astype(BF16)

    merged = []
    for off in (0, 1, PW, PW + 1):
        merged.append(dot_nt((token == base + off).astype(BF16), stream)[:, :E])
    local = sum(jnp.sum(m, axis=-1, keepdims=True) for m in merged)
    local_mean = local / (4 * E)
    spread = sum(jnp.sum((m - local_mean) * (m - local_mean), axis=-1, keepdims=True) for m in merged)
    statsend[...] = columns_to_lanes(local, spread, M)
    for i in range(1, T):
        send(to_tp(statsend, statbox.at[me], st_s.at[i - 1], st_r.at[me], lax.rem(me + i, T)))
    statbox[me] = statsend[...]
    for i in range(1, T):
        slot = lax.rem(me + i, T)
        to_tp(statsend, statbox.at[slot], st_s.at[0], st_r.at[slot], me).wait_recv()
    stats = [statbox[t] for t in range(T)]
    mean_row = sum(s[0:1] for s in stats) / (4 * D)
    square_row = sum(s[1:2] for s in stats) + (4 * E) * sum(
        (s[0:1] / (4 * E) - mean_row) * (s[0:1] / (4 * E) - mean_row) for s in stats
    )
    stat_cols = rows_to_columns(mean_row, lax.rsqrt(square_row / (4 * D) + EPS_LN), 128)[:M]
    row_mean, row_scale = stat_cols[:, 0:1], stat_cols[:, 1:2]
    for n in range(4):
        normal[n] = (
            (merged[n] - row_mean) * row_scale * ln_w[n:n + 1, :] + ln_b[n:n + 1, :]
        ).astype(BF16)

    wcopies[2].wait()
    for c in range(CH):
        lo = 2 * W * c
        part = sum(
            jnp.dot(normal[n], wm[n, :, lo:lo + 2 * W], preferred_element_type=F32)
            for n in range(4)
        )
        for k in range(T):
            rows = part[k * MD:(k + 1) * MD]
            sb3[c, k] = jnp.concatenate([rows[:, :W], rows[:, W:]], axis=0).astype(BF16)
        rb3[c, me] = sb3[c, me]
        for i in range(1, T):
            peer = lax.rem(me + i, T)
            send(to_tp(sb3.at[c, peer], rb3.at[c, me], m_s.at[c, i - 1], m_r.at[c, me], peer))

    spot = (lax.rem(iota((MD, 128), 1), MD) == iota((MD, 128), 0)).astype(F32)
    ids_row = jnp.dot(
        jnp.broadcast_to(own_ref[pl.ds(grp, 1), :].astype(F32), (128, MD)), spot,
        preferred_element_type=F32,
    )
    ids = jnp.transpose(ids_row)[:MD]
    lane = iota((MD, 128), 1)
    earlier = (ids == ids_row[:MD]) & (iota((MD, 128), 0) < lax.rem(lane, MD))
    rank = jnp.sum(earlier.astype(F32), axis=0, keepdims=True)
    N = 2 * CH
    rows = iota((G * 4 * N, 128), 0)
    lane = iota((G * 4 * N, 128), 1)
    pick = (
        (ids_row[0:1] == (rows // (4 * N)).astype(F32))
        & (rank == lax.rem(rows, 4).astype(F32))
        & (lane // MD == lax.rem(rows, 4 * N) // 4)
    )
    pick = pick.astype(BF16)[:, :N * MD]
    alive = live[pl.ds(pl.multiple_of(me * MD, MD), MD), :][:, 0:1]
    pieces = []
    for c in range(CH):
        for i in range(1, T):
            slot = lax.rem(me + i, T)
            to_tp(sb3.at[c, slot], rb3.at[c, slot], m_s.at[c, 0], m_r.at[c, slot], me).wait_recv()
        total = rb3[c, 0].astype(F32)
        for k in range(1, T):
            total = total + rb3[c, k].astype(F32)
        for h in range(2):
            at = (2 * c + h) * W
            x = total[h * MD:(h + 1) * MD] + bm[at:at + W].reshape(1, W)
            pieces.append(0.5 * x * (1.0 + lax.erf(x * (0.5 ** 0.5))) * alive)
    stacked = jnp.concatenate(pieces, axis=0).astype(BF16)
    ob[...] = jnp.dot(pick, stacked, preferred_element_type=F32).reshape(G, 4 * N, W).astype(BF16)
    for i in range(1, G):
        peer = lax.rem(grp + i, G)
        copy = pltpu.make_async_remote_copy(
            src_ref=ob.at[peer], dst_ref=rbo.at[grp], send_sem=o_s.at[i - 1],
            recv_sem=o_r.at[grp], device_id={"req": peer}, device_id_type=MESH,
        )
        copy.start()
        sends.append(copy)
    rbo[grp] = ob[grp]
    for i in range(1, G):
        slot = lax.rem(grp + i, G)
        pltpu.make_async_remote_copy(
            src_ref=ob.at[slot], dst_ref=rbo.at[slot], send_sem=o_s.at[0],
            recv_sem=o_r.at[slot], device_id={"req": grp}, device_id_type=MESH,
        ).wait_recv()
    got = [rbo[g].astype(F32) for g in range(G)]
    for c in range(out.shape[0]):
        for q in range(N):
            out[c, :, q * W:(q + 1) * W] = jnp.concatenate(
                [x[4 * q + c:4 * q + c + 1] for x in got], axis=0
            ).astype(BF16)
    for copy in sends:
        copy.wait_send()


def per_device(
    tokens, segments, norm_gain, wqkv, qk_gain, wproj, bproj, layer_scale,
    ln_weight, ln_bias, w_merge, b_merge, owners,
):
    T = lax.axis_size("tp")
    G = lax.axis_size("req")
    A = 4
    B = T // A
    R, D = tokens.shape[1:]
    S = R * T
    F = wqkv.shape[2]
    E = bproj.shape[0]
    EP = -(-E // 16) * 16
    M = S // 4
    MD = M // T
    PF = w_merge.shape[2]
    CH = 2
    W = PF // CH // 2
    capacity = (MD + G - 1) // G + 1
    C = 2
    dims = (A, B, T, R, G, E, EP, S, D, M, PF, CH)
    vmem = pl.BlockSpec(memory_space=pltpu.VMEM)
    hbm = pl.BlockSpec(memory_space=pl.ANY)
    dma = pltpu.SemaphoreType.DMA
    out = pl.pallas_call(
        functools.partial(body, dims),
        out_shape=jax.ShapeDtypeStruct((capacity, G, PF), BF16),
        in_specs=[vmem] * 10 + [hbm] * 3,
        out_specs=vmem,
        scratch_shapes=[
            pltpu.VMEM((3, D, F), BF16),
            pltpu.VMEM((F, D), BF16),
            pltpu.VMEM((4, E, PF), BF16),
            pltpu.VMEM((D, F), F32),
            pltpu.VMEM((T, EP, F), BF16),
            pltpu.VMEM((EP, 8), F32),
            pltpu.VMEM((T, C, R // C, D), BF16),
            pltpu.VMEM((T, R, D), BF16),
            pltpu.VMEM((3, T, R, F), F32),
            pltpu.VMEM((S, F), BF16),
            pltpu.VMEM((B - 1, A, EP, S), BF16),
            pltpu.VMEM((B - 1, A, EP, S), BF16),
            pltpu.VMEM((A - 1, EP, S), BF16),
            pltpu.VMEM((A - 1, EP, S), BF16),
            pltpu.VMEM((EP, S), F32),
            pltpu.VMEM((T, 8, S), F32),
            pltpu.VMEM((8, S), F32),
            pltpu.VMEM((T, 8, 128), F32),
            pltpu.VMEM((8, 128), F32),
            pltpu.VMEM((4, M, E), BF16),
            pltpu.VMEM((CH, T, 2 * MD, W), BF16),
            pltpu.VMEM((CH, T, 2 * MD, W), BF16),
            pltpu.VMEM((M, 128), F32),
            pltpu.VMEM((G, 8 * CH, W), BF16),
            pltpu.VMEM((G, 8 * CH, W), BF16),
            pltpu.VMEM((F // HD, S, S), F32),
            dma((3,)),
            dma((C, A - 1)), dma((C, A * (B - 1))), dma((T, C)),
            dma((T - 1,)), dma((T,)),
            dma((B - 1, A)), dma((B - 1, A)),
            dma((A - 1,)), dma((A - 1,)),
            dma((T - 1,)), dma((T,)),
            dma((CH, T - 1)), dma((CH, T)),
            dma((G - 1,)), dma((G,)),
        ],
        compiler_params=pltpu.CompilerParams(
            collective_id=0, has_side_effects=True, vmem_limit_bytes=56 * 1024 * 1024
        ),
    )(
        tokens.reshape(C, R // C, D), segments, norm_gain, qk_gain, bproj, layer_scale,
        ln_weight, ln_bias, b_merge, owners[:, :, 0], wqkv, wproj, w_merge,
    )
    return out.transpose(1, 0, 2).reshape(1, G, 1, capacity, PF)


def solution(mesh):
    placed = (
        P("req", "tp", None),
        P("req", None),
        P(),
        P(None, None, "tp"),
        P(None, "tp"),
        P("tp", None),
        P("tp"),
        P("tp"),
        P(None, "tp"),
        P(None, "tp"),
        P(None, "tp", None),
        P(),
        P(None, "tp", None),
    )
    return jax.shard_map(
        per_device,
        mesh=mesh,
        in_specs=placed,
        out_specs=P("req", None, "tp", None, None),
        check_vma=False,
    )
```
